32 devices in a mesh: req: 8 (over z, y), tp: 4 (over x, core).
Axes of the slice: x: 2, y: 2, z: 4, core: 2. Of those that a mesh axis runs over, the one named last changes fastest.
Arguments:
- tokens: bfloat16 [4096, 4096], P('req', 'tp'), may hold values from -400 to 400
- input_norm_gain: float32 [4096], replicated, may hold values from 0.1 to 1.9
- query_weight: bfloat16 [4096, 2048], P(None, 'tp'), may hold values from -0.078125 to 0.078125
- key_weight: bfloat16 [4096, 2048], P(None, 'tp'), may hold values from -1.953125 to 1.953125
- value_weight: bfloat16 [4096, 2048], P(None, 'tp'), may hold values from -0.09375 to 0.09375
- query_down_maps: bfloat16 [4096, 512], replicated, may hold values from -0.09375 to 0.09375
- value_down_maps: bfloat16 [4096, 512], replicated, may hold values from -0.09375 to 0.09375
- query_up_maps: bfloat16 [512, 2048], P(None, 'tp'), may hold values from -1.5 to 1.5
- value_up_maps: bfloat16 [512, 2048], P(None, 'tp'), may hold values from -1.5 to 1.5
- lengths: int32 [4], replicated, may hold values from 1 to 2304, 4096 in all
- prompt_adapter_index: int32 [4], replicated, may hold values from 0 to 31
Outputs:
- attended: bfloat16 [4096, 2048], P('req', 'tp')
The draws below stay inside these ranges and needn't reach their ends.
Inputs may be any that keep to these rules, and one draw needn't show every extreme that they name: `lengths`: the longest prompt has exactly 2304 tokens.
All inputs are finite; a program needn't handle non-finite values.
Results may differ from the reference program's by a relative error of at most 0.0083.
Values may be sent and summed in bfloat16 or wider, within the bound.
A program may use at most 192 MiB of HBM per device.

```python
import math
import jax
import jax.numpy as jnp
import numpy as np
from jax import lax

INPUT_WIDTH = 4096
HEADS = 16
HEAD = 128
ADAPTER_RANK = 16
ADAPTER_COUNT = 32
TOK_DEV = 512
HEAD_FEATURES = 2048
TOKENS = 4096
REQS = 4
MAXLEN = 2304


def weight_common(key):
    return jnp.clip(jax.random.normal(key, (INPUT_WIDTH, HEAD_FEATURES), jnp.float32), -5.0, 5.0) / math.sqrt(INPUT_WIDTH)


def draw_query_weight(key, part):
    return weight_common(jax.random.fold_in(key, 11)).astype(jnp.bfloat16)


def draw_key_weight(key, part):
    return weight_common(jax.random.fold_in(key, 12)).astype(jnp.bfloat16)


def draw_tokens(key, part):
    base_key = jax.random.fold_in(key, 21)
    feature_key = jax.random.fold_in(key, 22)
    row_key = jax.random.fold_in(key, 23)
    feature_scale = jnp.exp(jax.random.uniform(feature_key, (INPUT_WIDTH,), jnp.float32) * math.log(10.0))
    row_scale = jnp.exp(jax.random.uniform(row_key, (TOKENS, 1), jnp.float32) * math.log(10.0))
    base = jnp.clip(jax.random.normal(base_key, (TOKENS, INPUT_WIDTH), jnp.float32), -4.0, 4.0)
    return (base * feature_scale[None, :] * row_scale).astype(jnp.bfloat16)


def with_ends(drawn, key, smallest, high):
    extent = drawn.shape
    place = [jax.random.randint(jax.random.fold_in(key, axis), (), 0, extent[axis]) for axis in range(len(extent))]
    drawn = drawn.at[tuple(place)].set(smallest)
    longest = extent.index(max(extent))
    place[longest] = (place[longest] + 1) % extent[longest]
    return drawn.at[tuple(place)].set(high)


def block_levels(own_key, shape, pieces, smallest, high):
    level, own = 1.0, jax.random.fold_in(own_key, 6)
    for dim, parts in pieces:
        draws = jnp.exp(jax.random.uniform(jax.random.fold_in(own, dim), (parts,), jnp.float32, smallest / len(pieces), high / len(pieces)))
        level = level * jnp.repeat(draws, shape[dim] // parts).reshape([-1 if axis == dim else 1 for axis in range(len(shape))])
    return level


def split_up(count, total, reach, skew):
    weights = [(1 << 20) // math.isqrt(standing ** skew) + 1 for standing in range(2, count + 1)]
    surplus, counts = total - reach - (count - 1), [1] * (count - 1)
    while surplus > 0:
        free = [i for i in range(count - 1) if counts[i] < reach]
        whole, budget = sum([weights[i] for i in free]), surplus
        for i in free:
            addition = min(reach - counts[i], max(1, budget * weights[i] // whole), surplus)
            counts[i] = counts[i] + addition
            surplus = surplus - addition
    return np.array([reach] + counts)


def uneven_parts(own_key, number_of, total, bound, slope):
    if number_of == 2:
        one = jax.random.randint(own_key, (), max(1, total - bound), min(bound, total - 1) + 1)
        return jnp.stack([one, total - one])
    sizes = jnp.asarray(split_up(number_of, total, bound, slope), jnp.int32)
    twos = (number_of - 1) // 2
    donor, sink = sizes[1:1 + 2 * twos:2], sizes[2:2 + 2 * twos:2]
    slack = jnp.minimum(donor - 1, bound - sink)
    passed = jax.random.randint(jax.random.fold_in(own_key, 1), (twos,), 0, 1 << 20) % (slack + 1)
    sizes = sizes.at[1:1 + 2 * twos:2].set(donor - passed).at[2:2 + 2 * twos:2].set(sink + passed)
    return sizes[jax.random.permutation(jax.random.fold_in(own_key, 2), number_of)]


def noise(own_key, shape, scale, most, pieces=(), kind=jnp.bfloat16):
    drawn = scale * jax.random.normal(own_key, shape, jnp.float32)
    if pieces:
        drawn = drawn * block_levels(own_key, shape, pieces, -0.22, 0.18)
    return jnp.clip(drawn, -most, most).astype(kind)


def setup_inputs(seed: int = 0) -> dict:
    seeds = jax.random.split(jax.random.key(seed), 12)
    tokens = draw_tokens(jax.random.fold_in(seeds[11], 71), 0)
    input_norm_gain = jnp.clip(1.0 + 0.18 * jax.random.normal(seeds[1], (INPUT_WIDTH,), jnp.float32), 0.1, 1.9)
    query_weight = draw_query_weight(jax.random.fold_in(seeds[11], 71), 0)
    key_weight = draw_key_weight(jax.random.fold_in(seeds[11], 71), 0)
    value_weight = noise(seeds[4], (INPUT_WIDTH, HEAD_FEATURES), INPUT_WIDTH ** -0.5, 0.09375, ((1, 4),))
    query_down_maps = noise(seeds[5], (INPUT_WIDTH, ADAPTER_COUNT * ADAPTER_RANK), INPUT_WIDTH ** -0.5, 0.09375)
    value_down_maps = noise(seeds[6], (INPUT_WIDTH, ADAPTER_COUNT * ADAPTER_RANK), INPUT_WIDTH ** -0.5, 0.09375)
    query_up_maps = noise(seeds[7], (ADAPTER_COUNT * ADAPTER_RANK, HEAD_FEATURES), ADAPTER_RANK ** -0.5, 1.5, ((1, 4),))
    value_up_maps = noise(seeds[8], (ADAPTER_COUNT * ADAPTER_RANK, HEAD_FEATURES), ADAPTER_RANK ** -0.5, 1.5, ((1, 4),))
    lengths = uneven_parts(seeds[9], REQS, TOKENS, MAXLEN, 2).astype(jnp.int32)
    prompt_adapter_index = with_ends(jax.random.randint(seeds[10], (REQS,), 0, ADAPTER_COUNT), jax.random.fold_in(seeds[10], 1), 0, ADAPTER_COUNT - 1).astype(jnp.int32)
    return {"tokens": tokens, "input_norm_gain": input_norm_gain, "query_weight": query_weight, "key_weight": key_weight, "value_weight": value_weight, "query_down_maps": query_down_maps, "value_down_maps": value_down_maps, "query_up_maps": query_up_maps, "value_up_maps": value_up_maps, "lengths": lengths, "prompt_adapter_index": prompt_adapter_index}


EPS = 1e-05
ADAPTER_SCALE = 0.5
MASKED = -1e+30

def prompt_layout(lengths, positions):
    ends = jnp.cumsum(lengths).astype(jnp.int32)
    before = (ends[None, :] <= positions[:, None]).astype(jnp.int32)
    starts = lax.optimization_barrier(jnp.sum(before * lengths[None, :], axis=1)).astype(jnp.int32)
    prompt = lax.optimization_barrier(jnp.sum(before, axis=1)).astype(jnp.int32)
    return (starts, prompt)

def adapter_mask(prompt, prompt_adapter_index, count, rank):
    chosen = (prompt[:, None] == jnp.arange(prompt_adapter_index.shape[0], dtype=jnp.int32)[None, :]).astype(jnp.int32)
    adapter = lax.optimization_barrier(jnp.sum(chosen * prompt_adapter_index[None, :], axis=1)).astype(jnp.int32)
    column = jnp.arange(count * rank, dtype=jnp.int32) // rank
    return (column[None, :] == adapter[:, None]).astype(jnp.float32)

def rotate(field, offsets, width):
    half = width // 2
    freq = jnp.exp(jnp.arange(half, dtype=jnp.float32) * (-2.0 * math.log(10000.0) / width))
    angle = offsets.astype(jnp.float32)[:, None] * freq[None, :]
    cosine = jnp.cos(angle)[:, None, :]
    sine = jnp.sin(angle)[:, None, :]
    first = field[..., :half]
    second = field[..., half:]
    return jnp.concatenate([first * cosine - second * sine, second * cosine + first * sine], axis=-1)

def reference(tokens, input_norm_gain, query_weight, key_weight, value_weight, query_down_maps, value_down_maps, query_up_maps, value_up_maps, lengths, prompt_adapter_index):
    positions = jnp.arange(TOKENS, dtype=jnp.int32)
    starts, prompt = prompt_layout(lengths, positions)
    causal_mask = adapter_mask(prompt, prompt_adapter_index, ADAPTER_COUNT, ADAPTER_RANK)
    tok_float = tokens.astype(jnp.float32)
    normed = (tok_float * lax.rsqrt(lax.optimization_barrier(jnp.mean(tok_float * tok_float, axis=1, keepdims=True)) + EPS) * input_norm_gain[None, :]).astype(jnp.bfloat16)

    def apply_projection(weight):
        return jnp.dot(normed, weight, preferred_element_type=jnp.float32)
    query_middle = (apply_projection(query_down_maps) * causal_mask).astype(jnp.bfloat16)
    value_middle = (apply_projection(value_down_maps) * causal_mask).astype(jnp.bfloat16)
    query_linear = apply_projection(query_weight) + ADAPTER_SCALE * jnp.dot(query_middle, query_up_maps, preferred_element_type=jnp.float32)
    key_lin = apply_projection(key_weight)
    value_rows = (apply_projection(value_weight) + ADAPTER_SCALE * jnp.dot(value_middle, value_up_maps, preferred_element_type=jnp.float32)).astype(jnp.bfloat16)
    offsets = positions - starts
    queries = rotate(query_linear.reshape(TOKENS, HEADS, HEAD), offsets, HEAD).astype(jnp.bfloat16)
    keys = rotate(key_lin.reshape(TOKENS, HEADS, HEAD), offsets, HEAD).astype(jnp.bfloat16)
    value_rows = value_rows.reshape(TOKENS, HEADS, HEAD)
    padding = jnp.zeros((MAXLEN, HEADS, HEAD), jnp.bfloat16)
    keys_pad = jnp.concatenate([padding, keys], axis=0)
    values_pad = jnp.concatenate([padding, value_rows], axis=0)
    scale = 1.0 / math.sqrt(HEAD)

    def block(index):
        first = (index * TOK_DEV).astype(jnp.int32)
        query_block = lax.dynamic_slice_in_dim(queries, first, TOK_DEV, 0).astype(jnp.float32)
        key_block = lax.dynamic_slice_in_dim(keys_pad, first, MAXLEN + TOK_DEV, 0).astype(jnp.float32)
        value_block = lax.dynamic_slice_in_dim(values_pad, first, MAXLEN + TOK_DEV, 0).astype(jnp.float32)
        query_pos = first + jnp.arange(TOK_DEV, dtype=jnp.int32)
        query_start = lax.dynamic_slice_in_dim(starts, first, TOK_DEV, 0)
        key_pos = first - MAXLEN + jnp.arange(MAXLEN + TOK_DEV, dtype=jnp.int32)
        allowed = (key_pos[None, :] >= query_start[:, None]) & (key_pos[None, :] <= query_pos[:, None])
        scores = jnp.einsum('qhd,khd->hqk', query_block, key_block, precision=lax.Precision.HIGHEST) * scale
        scores = jnp.where(allowed[None], scores, MASKED)
        peak = lax.optimization_barrier(jnp.max(scores, axis=2, keepdims=True))
        weights = jnp.where(allowed[None], jnp.exp(scores - peak), 0.0)
        total = lax.optimization_barrier(jnp.sum(weights, axis=2))
        rounded = lax.optimization_barrier(weights.astype(jnp.bfloat16)).astype(jnp.float32)
        summed = jnp.einsum('hqk,khd->qhd', rounded, value_block, precision=lax.Precision.HIGHEST)
        return (summed / jnp.transpose(total)[:, :, None]).reshape(TOK_DEV, HEADS * HEAD).astype(jnp.bfloat16)
    result = lax.map(block, jnp.arange(TOKENS // TOK_DEV, dtype=jnp.int32))
    return result.reshape(TOKENS, HEADS * HEAD)
```

```python
import math

import jax
import jax.numpy as jnp
from jax import lax
from jax.experimental import pallas as pl
from jax.experimental.pallas import tpu as pltpu
from jax.sharding import PartitionSpec as P

HEAD = 128
ADAPTER_RANK = 16
ADAPTER_COUNT = 32


EPS = 1e-05
ADAPTER_SCALE = 0.5
MASKED = -1e30


def prompt_layout(lengths, positions):
    ends = jnp.cumsum(lengths)
    before = (ends[None, :] <= positions[:, None]).astype(jnp.int32)
    starts = jnp.sum(before * lengths[None, :], axis=1)
    prompt = jnp.sum(before, axis=1)
    return (starts, prompt)


def adapter_mask(prompt, prompt_adapter_index, count, rank):
    chosen = (
        prompt[:, None] == jnp.arange(prompt_adapter_index.shape[0], dtype=jnp.int32)[None, :]
    ).astype(jnp.int32)
    adapter = jnp.sum(chosen * prompt_adapter_index[None, :], axis=1)
    column = jnp.arange(count * rank, dtype=jnp.int32) // rank
    return (column[None, :] == adapter[:, None]).astype(jnp.float32)


def rotate(field, offsets, width):
    half = width // 2
    freq = jnp.exp(jnp.arange(half, dtype=jnp.float32) * (-2.0 * math.log(10000.0) / width))
    angle = offsets.astype(jnp.float32)[:, None] * freq[None, :]
    cosine = jnp.cos(angle)[:, None, :]
    sine = jnp.sin(angle)[:, None, :]
    first = field[..., :half]
    second = field[..., half:]
    return jnp.concatenate(
        [first * cosine - second * sine, second * cosine + first * sine], axis=-1
    )


def body(
    tokens,
    input_norm_gain,
    query_weight,
    key_weight,
    value_weight,
    query_down_maps,
    value_down_maps,
    query_up_maps,
    value_up_maps,
    lengths,
    prompt_adapter_index,
):
    row_count = tokens.shape[0]
    req_index = lax.axis_index("req")
    positions = req_index * row_count + jnp.arange(row_count, dtype=jnp.int32)
    starts, prompt = prompt_layout(lengths, positions)
    causal_mask = adapter_mask(prompt, prompt_adapter_index, ADAPTER_COUNT, ADAPTER_RANK)
    incoming_weights = (query_weight, key_weight, value_weight, query_down_maps, value_down_maps)
    whole = lax.all_gather(tokens, "tp", axis=1, tiled=True)
    whole_float = whole.astype(jnp.float32)
    normed = (
        whole_float
        * lax.rsqrt(jnp.mean(whole_float * whole_float, axis=1, keepdims=True) + EPS)
        * input_norm_gain[None, :]
    ).astype(jnp.bfloat16)
    projected = tuple(
        (jnp.dot(normed, weight, preferred_element_type=jnp.float32) for weight in incoming_weights)
    )
    query_linear, key_lin, value_linear, query_middle, value_middle = projected
    query_middle = (query_middle * causal_mask).astype(jnp.bfloat16)
    value_middle = (value_middle * causal_mask).astype(jnp.bfloat16)
    query_linear = query_linear + ADAPTER_SCALE * jnp.dot(
        query_middle, query_up_maps, preferred_element_type=jnp.float32
    )
    value_rows = (
        value_linear
        + ADAPTER_SCALE * jnp.dot(value_middle, value_up_maps, preferred_element_type=jnp.float32)
    ).astype(jnp.bfloat16)
    head_count = query_linear.shape[1] // HEAD
    offsets = positions - starts
    queries = jnp.transpose(
        rotate(query_linear.reshape(row_count, head_count, HEAD), offsets, HEAD).astype(
            jnp.bfloat16
        ),
        (1, 0, 2),
    )
    keys = (
        rotate(key_lin.reshape(row_count, head_count, HEAD), offsets, HEAD)
        .astype(jnp.bfloat16)
        .reshape(row_count, head_count * HEAD)
    )
    key_value = jnp.stack([keys, value_rows])
    scale = 1.0 / math.sqrt(HEAD)

    def attend(state, block, key_first):
        peak, total, summed = state
        block_rows = block.shape[1]
        key_block = block[0].reshape(block_rows, head_count, HEAD)
        value_block = block[1].reshape(block_rows, head_count, HEAD)
        scores = (
            jnp.einsum("hqd,khd->hqk", queries, key_block, preferred_element_type=jnp.float32)
            * scale
        )
        key_pos = key_first + jnp.arange(block_rows, dtype=jnp.int32)
        allowed = (key_pos[None, :] >= starts[:, None]) & (key_pos[None, :] <= positions[:, None])
        scores = jnp.where(allowed[None], scores, MASKED)
        new_peak = jnp.maximum(peak, jnp.max(scores, axis=2))
        weights = jnp.where(allowed[None], jnp.exp(scores - new_peak[:, :, None]), 0.0)
        factor = jnp.exp(peak - new_peak)
        new_total = total * factor + jnp.sum(weights, axis=2)
        new_summed = summed * factor[:, :, None] + jnp.einsum(
            "hqk,khd->hqd",
            weights.astype(jnp.bfloat16),
            value_block,
            preferred_element_type=jnp.float32,
        )
        return (new_peak, new_total, new_summed)

    def visit(state, block, key_first):
        return attend(state, block, key_first)

    initial = (
        jnp.full((head_count, row_count), MASKED, jnp.float32),
        jnp.zeros((head_count, row_count), jnp.float32),
        jnp.zeros((head_count, row_count, HEAD), jnp.float32),
    )
    piece = lax.all_gather(key_value, "req", axis=1, tiled=True)
    piece_rows = piece.shape[1]
    block_rows = row_count

    def inner(turn, carry):
        block = lax.dynamic_slice_in_dim(piece, turn * block_rows, block_rows, 1)
        return visit(carry, block, turn * block_rows)

    state = lax.fori_loop(0, piece_rows // block_rows, inner, initial)
    peak, total, summed = state
    attended = (summed / total[:, :, None]).astype(jnp.bfloat16)
    return jnp.transpose(attended, (1, 0, 2)).reshape(row_count, head_count * HEAD)


LOG2E = 1.4426950408889634
LAYERS = 4
COLUMNS = 2


def project_kernel(
    scalars,
    own,
    near,
    across,
    far,
    gain,
    cosine,
    sine,
    prompt_mask,
    query_w,
    key_w,
    value_w,
    down,
    query_up,
    value_up,
    out,
    normed,
    query_sum,
    key_sum,
    value_sum,
    down_sum,
):
    step = pl.program_id(0)
    blocks = (own, near, across, far)
    rows = own.shape[0]
    width = own.shape[1]

    @pl.when(step == 0)
    def _():
        part = 32

        def normalise(index, carry):
            at = pl.ds(pl.multiple_of(index * part, part), part)
            total = jnp.zeros((part, 1), jnp.float32)
            for block in blocks:
                value = block[at, :].astype(jnp.float32)
                total += jnp.sum(value * value, axis=1, keepdims=True)
            factor = lax.rsqrt(total / (len(blocks) * width) + EPS)
            for number, block in enumerate(blocks):
                value = block[at, :].astype(jnp.float32)
                normed[number, at, :] = (value * factor * gain[number]).astype(jnp.bfloat16)
            return carry

        lax.fori_loop(0, rows // part, normalise, 0)
        query_sum[...] = jnp.zeros_like(query_sum)
        key_sum[...] = jnp.zeros_like(key_sum)
        value_sum[...] = jnp.zeros_like(value_sum)
        down_sum[...] = jnp.zeros_like(down_sum)

    tile = normed[step]
    query_sum[...] += jnp.dot(tile, query_w[...], preferred_element_type=jnp.float32)
    key_sum[...] += jnp.dot(tile, key_w[...], preferred_element_type=jnp.float32)
    value_sum[...] += jnp.dot(tile, value_w[...], preferred_element_type=jnp.float32)
    down_sum[...] += jnp.dot(tile, down[...], preferred_element_type=jnp.float32)

    @pl.when(step == len(blocks) - 1)
    def _():
        layer = scalars[1]
        middle = (down_sum[...] * prompt_mask[...]).astype(jnp.bfloat16)
        for head in range(LAYERS):
            place = lax.rem(head - layer + LAYERS, LAYERS)
            lanes = slice(head * HEAD, (head + 1) * HEAD)
            query = query_sum[:, lanes] + ADAPTER_SCALE * jnp.dot(
                middle, query_up[:, lanes], preferred_element_type=jnp.float32
            )
            key = key_sum[:, lanes]
            value = value_sum[:, lanes] + ADAPTER_SCALE * jnp.dot(
                middle, value_up[:, lanes], preferred_element_type=jnp.float32
            )
            for slot, field in enumerate((query, key)):
                turned = field * cosine[...] + pltpu.roll(field, HEAD // 2, 1) * sine[...]
                out[place, slot] = turned.astype(jnp.bfloat16)
            out[place, 2] = value.astype(jnp.bfloat16)


def attend_kernel(scalars, mine, other, out, peak, total, summed):
    step = pl.program_id(0)
    rows = mine.shape[2]
    layer, column = scalars[0], scalars[1]
    prompts = scalars.shape[0] - 2
    query_block = lax.rem(layer - step + LAYERS, LAYERS) * COLUMNS + column
    first = query_block * rows
    last = first + rows - 1
    end = 0
    first_start = 0
    last_start = 0
    for prompt in range(prompts):
        length = scalars[2 + prompt]
        end = end + length
        first_start += jnp.where(end <= first, length, 0)
        last_start += jnp.where(end <= last, length, 0)
    query = mine[step, 0]
    peak[...] = jnp.full_like(peak, MASKED)
    total[...] = jnp.zeros_like(total)
    summed[...] = jnp.zeros_like(summed)
    scale = LOG2E / math.sqrt(HEAD)

    def visit(block, masked, key, value):
        scores = (
            lax.dot_general(
                query, key, (((1,), (1,)), ((), ())), preferred_element_type=jnp.float32
            )
            * scale
        )
        if masked:
            position = first + lax.broadcasted_iota(jnp.int32, (rows, 1), 0)
            start = jnp.zeros((rows, 1), jnp.int32)
            ending = 0
            for prompt in range(prompts):
                length = scalars[2 + prompt]
                ending = ending + length
                start += jnp.where(position >= ending, length, 0)
            key_position = block * rows + lax.broadcasted_iota(jnp.int32, (1, rows), 1)
            allowed = (key_position >= start) & (key_position <= position)
            scores = jnp.where(allowed, scores, MASKED)
        new_peak = jnp.maximum(peak[...], jnp.max(scores, axis=1, keepdims=True))
        weights = jnp.exp2(scores - new_peak)
        if masked:
            weights = jnp.where(allowed, weights, 0.0)
        factor = jnp.exp2(peak[...] - new_peak)
        total[...] = total[...] * factor + jnp.sum(weights, axis=1, keepdims=True)
        summed[...] = summed[...] * factor + jnp.dot(
            weights.astype(jnp.bfloat16), value, preferred_element_type=jnp.float32
        )
        peak[...] = new_peak

    def turn(block, carry):
        key_layer = block // COLUMNS
        place = lax.rem(layer - key_layer + LAYERS, LAYERS)
        same = lax.rem(block, COLUMNS) == column
        whole = (block < query_block) & (block * rows >= last_start)
        for is_mine in (True, False):
            for masked in (True, False):

                @pl.when((same == is_mine) & (whole != masked))
                def _():
                    if is_mine:
                        visit(block, masked, mine[place, 1], mine[place, 2])
                    else:
                        visit(block, masked, other[place, 0], other[place, 1])

        return carry

    lax.fori_loop(first_start // rows, query_block + 1, turn, 0)
    out[0] = (summed[...] / total[...]).astype(jnp.bfloat16)


def fast_body(
    tokens,
    input_norm_gain,
    query_weight,
    key_weight,
    value_weight,
    query_down_maps,
    value_down_maps,
    query_up_maps,
    value_up_maps,
    lengths,
    prompt_adapter_index,
):
    row_count, width = tokens.shape
    depth = query_weight.shape[0]
    features = query_weight.shape[1]
    prompts = lengths.shape[0]
    req_index = lax.axis_index("req")
    tp_index = lax.axis_index("tp")
    layer = req_index // COLUMNS
    column = lax.rem(req_index, COLUMNS)
    peers = depth // width

    def flip(array, bit):
        return lax.ppermute(array, "tp", [(i, i ^ bit) for i in range(peers)])

    across = flip(tokens, 2)
    near = flip(tokens, 1)
    far = flip(across, 1)

    positions = req_index * row_count + jnp.arange(row_count, dtype=jnp.int32)
    starts, prompt = prompt_layout(lengths, positions)
    lane = jnp.arange(2 * prompts * ADAPTER_RANK, dtype=jnp.int32)
    lane_prompt = lax.rem(lane // ADAPTER_RANK, prompts)
    prompt_mask = (prompt[:, None] == lane_prompt[None, :]).astype(jnp.float32)
    half = HEAD // 2
    freq = jnp.exp(jnp.arange(half, dtype=jnp.float32) * (-2.0 * math.log(10000.0) / HEAD))
    angle = (positions - starts).astype(jnp.float32)[:, None] * freq[None, :]
    cosine = jnp.cos(angle)
    sine = jnp.sin(angle)
    cosine = jnp.concatenate([cosine, cosine], axis=1)
    sine = jnp.concatenate([-sine, sine], axis=1)
    chosen = jnp.sum(
        (lane_prompt[:, None] == jnp.arange(prompts)[None, :]) * prompt_adapter_index[None, :],
        axis=1,
    ) * ADAPTER_RANK + lax.rem(lane, ADAPTER_RANK)
    pick = chosen[None, :] == jnp.arange(query_down_maps.shape[1])[:, None]
    is_query = lane < prompts * ADAPTER_RANK
    pick_query = (pick & is_query[None, :]).astype(jnp.bfloat16)
    pick_value = (pick & ~is_query[None, :]).astype(jnp.bfloat16)
    down = (
        jnp.dot(query_down_maps, pick_query, preferred_element_type=jnp.float32)
        + jnp.dot(value_down_maps, pick_value, preferred_element_type=jnp.float32)
    ).astype(jnp.bfloat16)
    query_up = jnp.dot(
        pick_query.T, query_up_maps, preferred_element_type=jnp.float32
    ).astype(jnp.bfloat16)
    value_up = jnp.dot(
        pick_value.T, value_up_maps, preferred_element_type=jnp.float32
    ).astype(jnp.bfloat16)
    order = tp_index ^ jnp.arange(peers, dtype=jnp.int32)
    gain = input_norm_gain.reshape(peers, 1, width)[order]

    def full(shape):
        return pl.BlockSpec(shape, lambda j, s: (0,) * len(shape))

    def weight(columns):
        return pl.BlockSpec((width, columns), lambda j, s: (s[0] ^ j, 0))

    projected = pl.pallas_call(
        project_kernel,
        grid_spec=pltpu.PrefetchScalarGridSpec(
            num_scalar_prefetch=1,
            grid=(peers,),
            in_specs=[full((row_count, width))] * 4
            + [full((peers, 1, width))]
            + [full((row_count, HEAD))] * 2
            + [full((row_count, lane.shape[0]))]
            + [weight(features)] * 3
            + [weight(lane.shape[0])]
            + [full((lane.shape[0], features))] * 2,
            out_specs=full((LAYERS, 3, row_count, HEAD)),
            scratch_shapes=[pltpu.VMEM((peers, row_count, width), jnp.bfloat16)]
            + [pltpu.VMEM((row_count, features), jnp.float32)] * 3
            + [pltpu.VMEM((row_count, lane.shape[0]), jnp.float32)],
        ),
        out_shape=jax.ShapeDtypeStruct((LAYERS, 3, row_count, HEAD), jnp.bfloat16),
        compiler_params=pltpu.CompilerParams(vmem_limit_bytes=48 * 1024 * 1024),
        name="project",
    )(
        jnp.stack([tp_index, layer]).astype(jnp.int32),
        tokens,
        near,
        across,
        far,
        gain,
        cosine,
        sine,
        prompt_mask,
        query_weight,
        key_weight,
        value_weight,
        down,
        query_up,
        value_up,
    )

    def along(array, distance):
        pairs = [
            (z * COLUMNS + y, (z + distance) % LAYERS * COLUMNS + y)
            for z in range(LAYERS)
            for y in range(COLUMNS)
        ]
        return lax.ppermute(array, "req", pairs)

    def swap(array):
        return lax.ppermute(array, "req", [(i, i ^ 1) for i in range(LAYERS * COLUMNS)])

    mine = [projected[0]]
    mine_kv = {s: along(projected[s, 1:], s) for s in (2, 1, 3)}
    mine_q = {s: along(projected[s, :1], s) for s in (2, 1, 3)}
    other = [swap(projected[0, 1:])] + [swap(mine_kv[s]) for s in range(1, LAYERS)]
    mine = jnp.stack(
        [projected[0]]
        + [jnp.concatenate([mine_q[s], mine_kv[s]], axis=0) for s in range(1, LAYERS)]
    )
    other = jnp.stack(other)
    attended = pl.pallas_call(
        attend_kernel,
        grid_spec=pltpu.PrefetchScalarGridSpec(
            num_scalar_prefetch=1,
            grid=(LAYERS,),
            in_specs=[
                full((LAYERS, 3, row_count, HEAD)),
                full((LAYERS, 2, row_count, HEAD)),
            ],
            out_specs=pl.BlockSpec((1, row_count, HEAD), lambda j, s: (j, 0, 0)),
            scratch_shapes=[
                pltpu.VMEM((row_count, 1), jnp.float32),
                pltpu.VMEM((row_count, 1), jnp.float32),
                pltpu.VMEM((row_count, HEAD), jnp.float32),
            ],
        ),
        out_shape=jax.ShapeDtypeStruct((LAYERS, row_count, HEAD), jnp.bfloat16),
        compiler_params=pltpu.CompilerParams(vmem_limit_bytes=48 * 1024 * 1024),
        name="attend",
    )(
        jnp.concatenate([jnp.stack([layer, column]).astype(jnp.int32), lengths]),
        mine,
        other,
    )
    parts = [attended[0]] + [along(attended[s], LAYERS - s) for s in range(1, LAYERS)]
    parts = jnp.stack(parts)
    slots = lax.rem(jnp.arange(LAYERS, dtype=jnp.int32) - layer + LAYERS, LAYERS)
    return jnp.concatenate([parts[slots[h]] for h in range(LAYERS)], axis=1)


def solution(mesh):
    in_specs = (
        P("req", "tp"),
        P(),
        P(None, "tp"),
        P(None, "tp"),
        P(None, "tp"),
        P(),
        P(),
        P(None, "tp"),
        P(None, "tp"),
        P(),
        P(),
    )
    out_specs = P("req", "tp")
    fast = mesh.shape["req"] == LAYERS * COLUMNS and mesh.shape["tp"] == 4
    chosen = fast_body if fast else body
    return jax.shard_map(
        chosen, mesh=mesh, in_specs=in_specs, out_specs=out_specs, check_vma=False
    )
```

```python
import math

import jax
import jax.numpy as jnp
from jax import lax
from jax.experimental import pallas as pl
from jax.experimental.pallas import tpu as pltpu
from jax.sharding import PartitionSpec as P

HEAD = 128
ADAPTER_RANK = 16
ADAPTER_COUNT = 32


EPS = 1e-05
ADAPTER_SCALE = 0.5
MASKED = -1e30


def prompt_layout(lengths, positions):
    ends = jnp.cumsum(lengths)
    before = (ends[None, :] <= positions[:, None]).astype(jnp.int32)
    starts = jnp.sum(before * lengths[None, :], axis=1)
    prompt = jnp.sum(before, axis=1)
    return (starts, prompt)


def adapter_mask(prompt, prompt_adapter_index, count, rank):
    chosen = (
        prompt[:, None] == jnp.arange(prompt_adapter_index.shape[0], dtype=jnp.int32)[None, :]
    ).astype(jnp.int32)
    adapter = jnp.sum(chosen * prompt_adapter_index[None, :], axis=1)
    column = jnp.arange(count * rank, dtype=jnp.int32) // rank
    return (column[None, :] == adapter[:, None]).astype(jnp.float32)


def rotate(field, offsets, width):
    half = width // 2
    freq = jnp.exp(jnp.arange(half, dtype=jnp.float32) * (-2.0 * math.log(10000.0) / width))
    angle = offsets.astype(jnp.float32)[:, None] * freq[None, :]
    cosine = jnp.cos(angle)[:, None, :]
    sine = jnp.sin(angle)[:, None, :]
    first = field[..., :half]
    second = field[..., half:]
    return jnp.concatenate(
        [first * cosine - second * sine, second * cosine + first * sine], axis=-1
    )


def body(
    tokens,
    input_norm_gain,
    query_weight,
    key_weight,
    value_weight,
    query_down_maps,
    value_down_maps,
    query_up_maps,
    value_up_maps,
    lengths,
    prompt_adapter_index,
):
    row_count = tokens.shape[0]
    req_index = lax.axis_index("req")
    positions = req_index * row_count + jnp.arange(row_count, dtype=jnp.int32)
    starts, prompt = prompt_layout(lengths, positions)
    causal_mask = adapter_mask(prompt, prompt_adapter_index, ADAPTER_COUNT, ADAPTER_RANK)
    incoming_weights = (query_weight, key_weight, value_weight, query_down_maps, value_down_maps)
    whole = lax.all_gather(tokens, "tp", axis=1, tiled=True)
    whole_float = whole.astype(jnp.float32)
    normed = (
        whole_float
        * lax.rsqrt(jnp.mean(whole_float * whole_float, axis=1, keepdims=True) + EPS)
        * input_norm_gain[None, :]
    ).astype(jnp.bfloat16)
    projected = tuple(
        (jnp.dot(normed, weight, preferred_element_type=jnp.float32) for weight in incoming_weights)
    )
    query_linear, key_lin, value_linear, query_middle, value_middle = projected
    query_middle = (query_middle * causal_mask).astype(jnp.bfloat16)
    value_middle = (value_middle * causal_mask).astype(jnp.bfloat16)
    query_linear = query_linear + ADAPTER_SCALE * jnp.dot(
        query_middle, query_up_maps, preferred_element_type=jnp.float32
    )
    value_rows = (
        value_linear
        + ADAPTER_SCALE * jnp.dot(value_middle, value_up_maps, preferred_element_type=jnp.float32)
    ).astype(jnp.bfloat16)
    head_count = query_linear.shape[1] // HEAD
    offsets = positions - starts
    queries = jnp.transpose(
        rotate(query_linear.reshape(row_count, head_count, HEAD), offsets, HEAD).astype(
            jnp.bfloat16
        ),
        (1, 0, 2),
    )
    keys = (
        rotate(key_lin.reshape(row_count, head_count, HEAD), offsets, HEAD)
        .astype(jnp.bfloat16)
        .reshape(row_count, head_count * HEAD)
    )
    key_value = jnp.stack([keys, value_rows])
    scale = 1.0 / math.sqrt(HEAD)

    def attend(state, block, key_first):
        peak, total, summed = state
        block_rows = block.shape[1]
        key_block = block[0].reshape(block_rows, head_count, HEAD)
        value_block = block[1].reshape(block_rows, head_count, HEAD)
        scores = (
            jnp.einsum("hqd,khd->hqk", queries, key_block, preferred_element_type=jnp.float32)
            * scale
        )
        key_pos = key_first + jnp.arange(block_rows, dtype=jnp.int32)
        allowed = (key_pos[None, :] >= starts[:, None]) & (key_pos[None, :] <= positions[:, None])
        scores = jnp.where(allowed[None], scores, MASKED)
        new_peak = jnp.maximum(peak, jnp.max(scores, axis=2))
        weights = jnp.where(allowed[None], jnp.exp(scores - new_peak[:, :, None]), 0.0)
        factor = jnp.exp(peak - new_peak)
        new_total = total * factor + jnp.sum(weights, axis=2)
        new_summed = summed * factor[:, :, None] + jnp.einsum(
            "hqk,khd->hqd",
            weights.astype(jnp.bfloat16),
            value_block,
            preferred_element_type=jnp.float32,
        )
        return (new_peak, new_total, new_summed)

    def visit(state, block, key_first):
        return attend(state, block, key_first)

    initial = (
        jnp.full((head_count, row_count), MASKED, jnp.float32),
        jnp.zeros((head_count, row_count), jnp.float32),
        jnp.zeros((head_count, row_count, HEAD), jnp.float32),
    )
    piece = lax.all_gather(key_value, "req", axis=1, tiled=True)
    piece_rows = piece.shape[1]
    block_rows = row_count

    def inner(turn, carry):
        block = lax.dynamic_slice_in_dim(piece, turn * block_rows, block_rows, 1)
        return visit(carry, block, turn * block_rows)

    state = lax.fori_loop(0, piece_rows // block_rows, inner, initial)
    peak, total, summed = state
    attended = (summed / total[:, :, None]).astype(jnp.bfloat16)
    return jnp.transpose(attended, (1, 0, 2)).reshape(row_count, head_count * HEAD)


LOG2E = 1.4426950408889634
LAYERS = 4
COLUMNS = 2


def project_kernel(
    scalars,
    own,
    near,
    across,
    far,
    gain,
    cosine,
    sine,
    prompt_mask,
    key_w,
    value_w,
    down,
    value_up,
    out,
    normed,
    key_sum,
    value_sum,
    down_sum,
):
    step = pl.program_id(0)
    blocks = (own, near, across, far)
    rows = own.shape[0]
    width = own.shape[1]

    @pl.when(step == 0)
    def _():
        part = 32

        def normalise(index, carry):
            at = pl.ds(pl.multiple_of(index * part, part), part)
            total = jnp.zeros((part, 1), jnp.float32)
            for block in blocks:
                value = block[at, :].astype(jnp.float32)
                total += jnp.sum(value * value, axis=1, keepdims=True)
            factor = lax.rsqrt(total / (len(blocks) * width) + EPS)
            for number, block in enumerate(blocks):
                value = block[at, :].astype(jnp.float32)
                normed[number, at, :] = (value * factor * gain[scalars[0] ^ number]).astype(jnp.bfloat16)
            return carry

        lax.fori_loop(0, rows // part, normalise, 0)
        key_sum[...] = jnp.zeros_like(key_sum)
        value_sum[...] = jnp.zeros_like(value_sum)
        down_sum[...] = jnp.zeros_like(down_sum)

    tile = normed[step]
    key_sum[...] += jnp.dot(tile, key_w[...], preferred_element_type=jnp.float32)
    value_sum[...] += jnp.dot(tile, value_w[...], preferred_element_type=jnp.float32)
    down_sum[...] += jnp.dot(tile, down[...], preferred_element_type=jnp.float32)

    @pl.when(step == len(blocks) - 1)
    def _():
        layer = scalars[1]
        middle = (down_sum[...] * prompt_mask[...]).astype(jnp.bfloat16)
        for head in range(LAYERS):
            place = lax.rem(head - layer + LAYERS, LAYERS)
            lanes = slice(head * HEAD, (head + 1) * HEAD)
            key = key_sum[:, lanes]
            value = value_sum[:, lanes] + ADAPTER_SCALE * jnp.dot(
                middle, value_up[:, lanes], preferred_element_type=jnp.float32
            )
            turned = key * cosine[...] + pltpu.roll(key, HEAD // 2, 1) * sine[...]
            out[place, 0] = turned.astype(jnp.bfloat16)
            out[place, 1] = value.astype(jnp.bfloat16)


def query_kernel(
    scalars, normed, cosine, sine, prompt_mask, query_w, down, query_up, out, query_sum, down_sum
):
    step = pl.program_id(0)

    @pl.when(step == 0)
    def _():
        query_sum[...] = jnp.zeros_like(query_sum)
        down_sum[...] = jnp.zeros_like(down_sum)

    tile = normed[0]
    query_sum[...] += jnp.dot(tile, query_w[...], preferred_element_type=jnp.float32)
    down_sum[...] += jnp.dot(tile, down[...], preferred_element_type=jnp.float32)

    @pl.when(step == pl.num_programs(0) - 1)
    def _():
        layer = scalars[1]
        middle = (down_sum[...] * prompt_mask[...]).astype(jnp.bfloat16)
        for head in range(LAYERS):
            place = lax.rem(head - layer + LAYERS, LAYERS)
            lanes = slice(head * HEAD, (head + 1) * HEAD)
            query = query_sum[:, lanes] + ADAPTER_SCALE * jnp.dot(
                middle, query_up[:, lanes], preferred_element_type=jnp.float32
            )
            turned = query * cosine[...] + pltpu.roll(query, HEAD // 2, 1) * sine[...]
            out[place] = turned.astype(jnp.bfloat16)


def attend_kernel(scalars, queries, mine, other, out, peak, total, summed):
    step = pl.program_id(0)
    rows = queries.shape[1]
    layer, column = scalars[0], scalars[1]
    prompts = scalars.shape[0] - 2
    query_block = lax.rem(layer - step + LAYERS, LAYERS) * COLUMNS + column
    first = query_block * rows
    last = first + rows - 1
    end = 0
    first_start = 0
    last_start = 0
    for prompt in range(prompts):
        length = scalars[2 + prompt]
        end = end + length
        first_start += jnp.where(end <= first, length, 0)
        last_start += jnp.where(end <= last, length, 0)
    query = queries[step]
    peak[...] = jnp.full_like(peak, MASKED)
    total[...] = jnp.zeros_like(total)
    summed[...] = jnp.zeros_like(summed)
    scale = LOG2E / math.sqrt(HEAD)

    def visit(block, masked, key, value):
        scores = (
            lax.dot_general(
                query, key, (((1,), (1,)), ((), ())), preferred_element_type=jnp.float32
            )
            * scale
        )
        if masked:
            position = first + lax.broadcasted_iota(jnp.int32, (rows, 1), 0)
            start = jnp.zeros((rows, 1), jnp.int32)
            ending = 0
            for prompt in range(prompts):
                length = scalars[2 + prompt]
                ending = ending + length
                start += jnp.where(position >= ending, length, 0)
            key_position = block * rows + lax.broadcasted_iota(jnp.int32, (1, rows), 1)
            allowed = (key_position >= start) & (key_position <= position)
            scores = jnp.where(allowed, scores, MASKED)
        new_peak = jnp.maximum(peak[...], jnp.max(scores, axis=1, keepdims=True))
        weights = jnp.exp2(scores - new_peak)
        if masked:
            weights = jnp.where(allowed, weights, 0.0)
        factor = jnp.exp2(peak[...] - new_peak)
        total[...] = total[...] * factor + jnp.sum(weights, axis=1, keepdims=True)
        summed[...] = summed[...] * factor + jnp.dot(
            weights.astype(jnp.bfloat16), value, preferred_element_type=jnp.float32
        )
        peak[...] = new_peak

    def turn(block, carry):
        key_layer = block // COLUMNS
        place = lax.rem(layer - key_layer + LAYERS, LAYERS)
        same = lax.rem(block, COLUMNS) == column
        whole = (block < query_block) & (block * rows >= last_start)
        for is_mine in (True, False):
            for masked in (True, False):

                @pl.when((same == is_mine) & (whole != masked))
                def _():
                    if is_mine:
                        visit(block, masked, mine[place, 0], mine[place, 1])
                    else:
                        visit(block, masked, other[place, 0], other[place, 1])

        return carry

    lax.fori_loop(first_start // rows, query_block + 1, turn, 0)
    out[0] = (summed[...] / total[...]).astype(jnp.bfloat16)


def fast_body(
    tokens,
    input_norm_gain,
    query_weight,
    key_weight,
    value_weight,
    query_down_maps,
    value_down_maps,
    query_up_maps,
    value_up_maps,
    lengths,
    prompt_adapter_index,
):
    row_count, width = tokens.shape
    depth = query_weight.shape[0]
    features = query_weight.shape[1]
    prompts = lengths.shape[0]
    req_index = lax.axis_index("req")
    tp_index = lax.axis_index("tp")
    layer = req_index // COLUMNS
    column = lax.rem(req_index, COLUMNS)
    peers = depth // width

    def flip(array, bit):
        return lax.ppermute(array, "tp", [(i, i ^ bit) for i in range(peers)])

    across = flip(tokens, 2)
    near = flip(tokens, 1)

    positions = req_index * row_count + jnp.arange(row_count, dtype=jnp.int32)
    starts, prompt = prompt_layout(lengths, positions)
    lane = jnp.arange(2 * prompts * ADAPTER_RANK, dtype=jnp.int32)
    lane_prompt = lax.rem(lane // ADAPTER_RANK, prompts)
    prompt_mask = (prompt[:, None] == lane_prompt[None, :]).astype(jnp.float32)
    half = HEAD // 2
    freq = jnp.exp(jnp.arange(half, dtype=jnp.float32) * (-2.0 * math.log(10000.0) / HEAD))
    angle = (positions - starts).astype(jnp.float32)[:, None] * freq[None, :]
    cosine = jnp.cos(angle)
    sine = jnp.sin(angle)
    cosine = jnp.concatenate([cosine, cosine], axis=1)
    sine = jnp.concatenate([-sine, sine], axis=1)
    chosen = jnp.sum(
        (lane_prompt[:, None] == jnp.arange(prompts)[None, :]) * prompt_adapter_index[None, :],
        axis=1,
    ) * ADAPTER_RANK + lax.rem(lane, ADAPTER_RANK)
    pick = chosen[None, :] == jnp.arange(query_down_maps.shape[1])[:, None]
    is_query = lane < prompts * ADAPTER_RANK
    pick_query = (pick & is_query[None, :]).astype(jnp.bfloat16)
    pick_value = (pick & ~is_query[None, :]).astype(jnp.bfloat16)
    down = (
        jnp.dot(query_down_maps, pick_query, preferred_element_type=jnp.float32)
        + jnp.dot(value_down_maps, pick_value, preferred_element_type=jnp.float32)
    ).astype(jnp.bfloat16)
    query_up = jnp.dot(
        pick_query.T, query_up_maps, preferred_element_type=jnp.float32
    ).astype(jnp.bfloat16)
    value_up = jnp.dot(
        pick_value.T, value_up_maps, preferred_element_type=jnp.float32
    ).astype(jnp.bfloat16)
    gain = input_norm_gain.reshape(peers, 1, width)
    across, gain, cosine, sine, prompt_mask, down, query_up, value_up = lax.optimization_barrier(
        (across, gain, cosine, sine, prompt_mask, down, query_up, value_up)
    )
    far = flip(across, 1)

    def full(shape):
        return pl.BlockSpec(shape, lambda j, s: (0,) * len(shape))

    def weight(columns):
        return pl.BlockSpec((width, columns), lambda j, s: (s[0] ^ j, 0))

    places = jnp.stack([tp_index, layer]).astype(jnp.int32)
    lanes = lane.shape[0]
    key_value, normed = pl.pallas_call(
        project_kernel,
        grid_spec=pltpu.PrefetchScalarGridSpec(
            num_scalar_prefetch=1,
            grid=(peers,),
            in_specs=[full((row_count, width))] * 4
            + [full((peers, 1, width))]
            + [full((row_count, HEAD))] * 2
            + [full((row_count, lanes))]
            + [weight(features)] * 2
            + [weight(lanes), full((lanes, features))],
            out_specs=[
                full((LAYERS, 2, row_count, HEAD)),
                full((peers, row_count, width)),
            ],
            scratch_shapes=[pltpu.VMEM((row_count, features), jnp.float32)] * 2
            + [pltpu.VMEM((row_count, lanes), jnp.float32)],
        ),
        out_shape=[
            jax.ShapeDtypeStruct((LAYERS, 2, row_count, HEAD), jnp.bfloat16),
            jax.ShapeDtypeStruct((peers, row_count, width), jnp.bfloat16),
        ],
        compiler_params=pltpu.CompilerParams(vmem_limit_bytes=48 * 1024 * 1024),
        name="project",
    )(
        places,
        tokens,
        near,
        across,
        far,
        gain,
        cosine,
        sine,
        prompt_mask,
        key_weight,
        value_weight,
        down,
        value_up,
    )
    queries = pl.pallas_call(
        query_kernel,
        grid_spec=pltpu.PrefetchScalarGridSpec(
            num_scalar_prefetch=1,
            grid=(peers,),
            in_specs=[pl.BlockSpec((1, row_count, width), lambda j, s: (j, 0, 0))]
            + [full((row_count, HEAD))] * 2
            + [full((row_count, lanes)), weight(features), weight(lanes)]
            + [full((lanes, features))],
            out_specs=full((LAYERS, row_count, HEAD)),
            scratch_shapes=[
                pltpu.VMEM((row_count, features), jnp.float32),
                pltpu.VMEM((row_count, lanes), jnp.float32),
            ],
        ),
        out_shape=jax.ShapeDtypeStruct((LAYERS, row_count, HEAD), jnp.bfloat16),
        compiler_params=pltpu.CompilerParams(vmem_limit_bytes=48 * 1024 * 1024),
        cost_estimate=pl.CostEstimate(
            flops=2 * row_count * depth * (features + lanes),
            bytes_accessed=2 * depth * (row_count + features),
            transcendentals=0,
        ),
        name="project_queries",
    )(places, normed, cosine, sine, prompt_mask, query_weight, down, query_up)

    def along(array, distance):
        pairs = [
            (z * COLUMNS + y, (z + distance) % LAYERS * COLUMNS + y)
            for z in range(LAYERS)
            for y in range(COLUMNS)
        ]
        return lax.ppermute(array, "req", pairs)

    def swap(array):
        return lax.ppermute(array, "req", [(i, i ^ 1) for i in range(LAYERS * COLUMNS)])

    arrived = {s: along(key_value[s], s) for s in (2, 1, 3)}
    other = jnp.stack([swap(key_value[0])] + [swap(arrived[s]) for s in range(1, LAYERS)])
    mine = jnp.stack([key_value[0]] + [arrived[s] for s in range(1, LAYERS)])
    queries = jnp.stack(
        [queries[0]] + [along(queries[s], s) for s in range(1, LAYERS)]
    )
    attended = pl.pallas_call(
        attend_kernel,
        grid_spec=pltpu.PrefetchScalarGridSpec(
            num_scalar_prefetch=1,
            grid=(LAYERS,),
            in_specs=[
                full((LAYERS, row_count, HEAD)),
                full((LAYERS, 2, row_count, HEAD)),
                full((LAYERS, 2, row_count, HEAD)),
            ],
            out_specs=pl.BlockSpec((1, row_count, HEAD), lambda j, s: (j, 0, 0)),
            scratch_shapes=[
                pltpu.VMEM((row_count, 1), jnp.float32),
                pltpu.VMEM((row_count, 1), jnp.float32),
                pltpu.VMEM((row_count, HEAD), jnp.float32),
            ],
        ),
        out_shape=jax.ShapeDtypeStruct((LAYERS, row_count, HEAD), jnp.bfloat16),
        compiler_params=pltpu.CompilerParams(vmem_limit_bytes=48 * 1024 * 1024),
        name="attend",
    )(
        jnp.concatenate([jnp.stack([layer, column]).astype(jnp.int32), lengths]),
        queries,
        mine,
        other,
    )
    parts = [attended[0]] + [along(attended[s], LAYERS - s) for s in range(1, LAYERS)]
    parts = jnp.stack(parts)
    slots = lax.rem(jnp.arange(LAYERS, dtype=jnp.int32) - layer + LAYERS, LAYERS)
    return jnp.concatenate([parts[slots[h]] for h in range(LAYERS)], axis=1)


def solution(mesh):
    in_specs = (
        P("req", "tp"),
        P(),
        P(None, "tp"),
        P(None, "tp"),
        P(None, "tp"),
        P(),
        P(),
        P(None, "tp"),
        P(None, "tp"),
        P(),
        P(),
    )
    out_specs = P("req", "tp")
    fast = mesh.shape["req"] == LAYERS * COLUMNS and mesh.shape["tp"] == 4
    chosen = fast_body if fast else body
    return jax.shard_map(
        chosen, mesh=mesh, in_specs=in_specs, out_specs=out_specs, check_vma=False
    )
```

```python
import math

import jax
import jax.numpy as jnp
from jax import lax
from jax.experimental import pallas as pl
from jax.experimental.pallas import tpu as pltpu
from jax.sharding import PartitionSpec as P

HEAD = 128
ADAPTER_RANK = 16
ADAPTER_COUNT = 32


EPS = 1e-05
ADAPTER_SCALE = 0.5
MASKED = -1e30


def prompt_layout(lengths, positions):
    ends = jnp.cumsum(lengths)
    before = (ends[None, :] <= positions[:, None]).astype(jnp.int32)
    starts = jnp.sum(before * lengths[None, :], axis=1)
    prompt = jnp.sum(before, axis=1)
    return (starts, prompt)


def adapter_mask(prompt, prompt_adapter_index, count, rank):
    chosen = (
        prompt[:, None] == jnp.arange(prompt_adapter_index.shape[0], dtype=jnp.int32)[None, :]
    ).astype(jnp.int32)
    adapter = jnp.sum(chosen * prompt_adapter_index[None, :], axis=1)
    column = jnp.arange(count * rank, dtype=jnp.int32) // rank
    return (column[None, :] == adapter[:, None]).astype(jnp.float32)


def rotate(field, offsets, width):
    half = width // 2
    freq = jnp.exp(jnp.arange(half, dtype=jnp.float32) * (-2.0 * math.log(10000.0) / width))
    angle = offsets.astype(jnp.float32)[:, None] * freq[None, :]
    cosine = jnp.cos(angle)[:, None, :]
    sine = jnp.sin(angle)[:, None, :]
    first = field[..., :half]
    second = field[..., half:]
    return jnp.concatenate(
        [first * cosine - second * sine, second * cosine + first * sine], axis=-1
    )


def body(
    tokens,
    input_norm_gain,
    query_weight,
    key_weight,
    value_weight,
    query_down_maps,
    value_down_maps,
    query_up_maps,
    value_up_maps,
    lengths,
    prompt_adapter_index,
):
    row_count = tokens.shape[0]
    req_index = lax.axis_index("req")
    positions = req_index * row_count + jnp.arange(row_count, dtype=jnp.int32)
    starts, prompt = prompt_layout(lengths, positions)
    causal_mask = adapter_mask(prompt, prompt_adapter_index, ADAPTER_COUNT, ADAPTER_RANK)
    incoming_weights = (query_weight, key_weight, value_weight, query_down_maps, value_down_maps)
    whole = lax.all_gather(tokens, "tp", axis=1, tiled=True)
    whole_float = whole.astype(jnp.float32)
    normed = (
        whole_float
        * lax.rsqrt(jnp.mean(whole_float * whole_float, axis=1, keepdims=True) + EPS)
        * input_norm_gain[None, :]
    ).astype(jnp.bfloat16)
    projected = tuple(
        (jnp.dot(normed, weight, preferred_element_type=jnp.float32) for weight in incoming_weights)
    )
    query_linear, key_lin, value_linear, query_middle, value_middle = projected
    query_middle = (query_middle * causal_mask).astype(jnp.bfloat16)
    value_middle = (value_middle * causal_mask).astype(jnp.bfloat16)
    query_linear = query_linear + ADAPTER_SCALE * jnp.dot(
        query_middle, query_up_maps, preferred_element_type=jnp.float32
    )
    value_rows = (
        value_linear
        + ADAPTER_SCALE * jnp.dot(value_middle, value_up_maps, preferred_element_type=jnp.float32)
    ).astype(jnp.bfloat16)
    head_count = query_linear.shape[1] // HEAD
    offsets = positions - starts
    queries = jnp.transpose(
        rotate(query_linear.reshape(row_count, head_count, HEAD), offsets, HEAD).astype(
            jnp.bfloat16
        ),
        (1, 0, 2),
    )
    keys = (
        rotate(key_lin.reshape(row_count, head_count, HEAD), offsets, HEAD)
        .astype(jnp.bfloat16)
        .reshape(row_count, head_count * HEAD)
    )
    key_value = jnp.stack([keys, value_rows])
    scale = 1.0 / math.sqrt(HEAD)

    def attend(state, block, key_first):
        peak, total, summed = state
        block_rows = block.shape[1]
        key_block = block[0].reshape(block_rows, head_count, HEAD)
        value_block = block[1].reshape(block_rows, head_count, HEAD)
        scores = (
            jnp.einsum("hqd,khd->hqk", queries, key_block, preferred_element_type=jnp.float32)
            * scale
        )
        key_pos = key_first + jnp.arange(block_rows, dtype=jnp.int32)
        allowed = (key_pos[None, :] >= starts[:, None]) & (key_pos[None, :] <= positions[:, None])
        scores = jnp.where(allowed[None], scores, MASKED)
        new_peak = jnp.maximum(peak, jnp.max(scores, axis=2))
        weights = jnp.where(allowed[None], jnp.exp(scores - new_peak[:, :, None]), 0.0)
        factor = jnp.exp(peak - new_peak)
        new_total = total * factor + jnp.sum(weights, axis=2)
        new_summed = summed * factor[:, :, None] + jnp.einsum(
            "hqk,khd->hqd",
            weights.astype(jnp.bfloat16),
            value_block,
            preferred_element_type=jnp.float32,
        )
        return (new_peak, new_total, new_summed)

    def visit(state, block, key_first):
        return attend(state, block, key_first)

    initial = (
        jnp.full((head_count, row_count), MASKED, jnp.float32),
        jnp.zeros((head_count, row_count), jnp.float32),
        jnp.zeros((head_count, row_count, HEAD), jnp.float32),
    )
    piece = lax.all_gather(key_value, "req", axis=1, tiled=True)
    piece_rows = piece.shape[1]
    block_rows = row_count

    def inner(turn, carry):
        block = lax.dynamic_slice_in_dim(piece, turn * block_rows, block_rows, 1)
        return visit(carry, block, turn * block_rows)

    state = lax.fori_loop(0, piece_rows // block_rows, inner, initial)
    peak, total, summed = state
    attended = (summed / total[:, :, None]).astype(jnp.bfloat16)
    return jnp.transpose(attended, (1, 0, 2)).reshape(row_count, head_count * HEAD)


LOG2E = 1.4426950408889634
LAYERS = 4
COLUMNS = 2


def project_kernel(
    scalars,
    own,
    near,
    across,
    far,
    gain,
    cosine,
    sine,
    prompt_mask,
    key_w,
    value_w,
    down,
    value_up,
    out,
    normed,
    key_sum,
    value_sum,
    down_sum,
):
    step = pl.program_id(0)
    blocks = (own, near, across, far)
    rows = own.shape[0]
    width = own.shape[1]

    @pl.when(step == 0)
    def _():
        part = 32

        def normalise(index, carry):
            at = pl.ds(pl.multiple_of(index * part, part), part)
            total = jnp.zeros((part, 1), jnp.float32)
            for block in blocks:
                value = block[at, :].astype(jnp.float32)
                total += jnp.sum(value * value, axis=1, keepdims=True)
            factor = lax.rsqrt(total / (len(blocks) * width) + EPS)
            for number, block in enumerate(blocks):
                value = block[at, :].astype(jnp.float32)
                normed[number, at, :] = (value * factor * gain[scalars[0] ^ number]).astype(jnp.bfloat16)
            return carry

        lax.fori_loop(0, rows // part, normalise, 0)
        key_sum[...] = jnp.zeros_like(key_sum)
        value_sum[...] = jnp.zeros_like(value_sum)
        down_sum[...] = jnp.zeros_like(down_sum)

    tile = normed[step]
    key_sum[...] += jnp.dot(tile, key_w[...], preferred_element_type=jnp.float32)
    value_sum[...] += jnp.dot(tile, value_w[...], preferred_element_type=jnp.float32)
    down_sum[...] += jnp.dot(tile, down[...], preferred_element_type=jnp.float32)

    @pl.when(step == len(blocks) - 1)
    def _():
        layer = scalars[1]
        middle = (down_sum[...] * prompt_mask[...]).astype(jnp.bfloat16)
        for head in range(LAYERS):
            place = lax.rem(head - layer + LAYERS, LAYERS)
            lanes = slice(head * HEAD, (head + 1) * HEAD)
            key = key_sum[:, lanes]
            value = value_sum[:, lanes] + ADAPTER_SCALE * jnp.dot(
                middle, value_up[:, lanes], preferred_element_type=jnp.float32
            )
            turned = key * cosine[...] + pltpu.roll(key, HEAD // 2, 1) * sine[...]
            out[place, 0] = turned.astype(jnp.bfloat16)
            out[place, 1] = value.astype(jnp.bfloat16)


def query_kernel(
    scalars, normed, cosine, sine, prompt_mask, query_w, down, query_up, out, query_sum, down_sum
):
    step = pl.program_id(0)

    @pl.when(step == 0)
    def _():
        query_sum[...] = jnp.zeros_like(query_sum)
        down_sum[...] = jnp.zeros_like(down_sum)

    tile = normed[0]
    query_sum[...] += jnp.dot(tile, query_w[...], preferred_element_type=jnp.float32)
    down_sum[...] += jnp.dot(tile, down[...], preferred_element_type=jnp.float32)

    @pl.when(step == pl.num_programs(0) - 1)
    def _():
        layer = scalars[1]
        middle = (down_sum[...] * prompt_mask[...]).astype(jnp.bfloat16)
        for head in range(LAYERS):
            place = lax.rem(head - layer + LAYERS, LAYERS)
            lanes = slice(head * HEAD, (head + 1) * HEAD)
            query = query_sum[:, lanes] + ADAPTER_SCALE * jnp.dot(
                middle, query_up[:, lanes], preferred_element_type=jnp.float32
            )
            turned = query * cosine[...] + pltpu.roll(query, HEAD // 2, 1) * sine[...]
            out[place] = turned.astype(jnp.bfloat16)


def attend_kernel(scalars, queries, mine, other, out, peak, total, summed):
    step = pl.program_id(0)
    rows = queries.shape[1]
    layer, column = scalars[0], scalars[1]
    prompts = scalars.shape[0] - 2
    query_block = lax.rem(layer - step + LAYERS, LAYERS) * COLUMNS + column
    first = query_block * rows
    last = first + rows - 1
    end = 0
    first_start = 0
    last_start = 0
    for prompt in range(prompts):
        length = scalars[2 + prompt]
        end = end + length
        first_start += jnp.where(end <= first, length, 0)
        last_start += jnp.where(end <= last, length, 0)
    query = queries[step]
    peak[...] = jnp.full_like(peak, MASKED)
    total[...] = jnp.zeros_like(total)
    summed[...] = jnp.zeros_like(summed)
    scale = LOG2E / math.sqrt(HEAD)

    def visit(block, masked, key, value):
        scores = (
            lax.dot_general(
                query, key, (((1,), (1,)), ((), ())), preferred_element_type=jnp.float32
            )
            * scale
        )
        if masked:
            position = first + lax.broadcasted_iota(jnp.int32, (rows, 1), 0)
            start = jnp.zeros((rows, 1), jnp.int32)
            ending = 0
            for prompt in range(prompts):
                length = scalars[2 + prompt]
                ending = ending + length
                start += jnp.where(position >= ending, length, 0)
            key_position = block * rows + lax.broadcasted_iota(jnp.int32, (1, rows), 1)
            allowed = (key_position >= start) & (key_position <= position)
            scores = jnp.where(allowed, scores, MASKED)
        new_peak = jnp.maximum(peak[...], jnp.max(scores, axis=1, keepdims=True))
        weights = jnp.exp2(scores - new_peak)
        if masked:
            weights = jnp.where(allowed, weights, 0.0)
        factor = jnp.exp2(peak[...] - new_peak)
        total[...] = total[...] * factor + jnp.sum(weights, axis=1, keepdims=True)
        summed[...] = summed[...] * factor + jnp.dot(
            weights.astype(jnp.bfloat16), value, preferred_element_type=jnp.float32
        )
        peak[...] = new_peak

    def turn(block, carry):
        key_layer = block // COLUMNS
        place = lax.rem(layer - key_layer + LAYERS, LAYERS)
        same = lax.rem(block, COLUMNS) == column
        whole = (block < query_block) & (block * rows >= last_start)
        for is_mine in (True, False):
            for masked in (True, False):

                @pl.when((same == is_mine) & (whole != masked))
                def _():
                    if is_mine:
                        visit(block, masked, mine[place, 0], mine[place, 1])
                    else:
                        visit(block, masked, other[place, 0], other[place, 1])

        return carry

    lax.fori_loop(first_start // rows, query_block + 1, turn, 0)
    out[0] = (summed[...] / total[...]).astype(jnp.bfloat16)


def fast_body(
    tokens,
    input_norm_gain,
    query_weight,
    key_weight,
    value_weight,
    query_down_maps,
    value_down_maps,
    query_up_maps,
    value_up_maps,
    lengths,
    prompt_adapter_index,
):
    row_count, width = tokens.shape
    depth = query_weight.shape[0]
    features = query_weight.shape[1]
    prompts = lengths.shape[0]
    req_index = lax.axis_index("req")
    tp_index = lax.axis_index("tp")
    layer = req_index // COLUMNS
    column = lax.rem(req_index, COLUMNS)
    peers = depth // width

    def flip(array, bit):
        return lax.ppermute(array, "tp", [(i, i ^ bit) for i in range(peers)])

    across = flip(tokens, 2)
    near = flip(tokens, 1)

    positions = req_index * row_count + jnp.arange(row_count, dtype=jnp.int32)
    starts, prompt = prompt_layout(lengths, positions)
    lane = jnp.arange(2 * prompts * ADAPTER_RANK, dtype=jnp.int32)
    lane_prompt = lax.rem(lane // ADAPTER_RANK, prompts)
    prompt_mask = (prompt[:, None] == lane_prompt[None, :]).astype(jnp.float32)
    half = HEAD // 2
    freq = jnp.exp(jnp.arange(half, dtype=jnp.float32) * (-2.0 * math.log(10000.0) / HEAD))
    angle = (positions - starts).astype(jnp.float32)[:, None] * freq[None, :]
    cosine = jnp.cos(angle)
    sine = jnp.sin(angle)
    cosine = jnp.concatenate([cosine, cosine], axis=1)
    sine = jnp.concatenate([-sine, sine], axis=1)
    chosen = jnp.sum(
        (lane_prompt[:, None] == jnp.arange(prompts)[None, :]) * prompt_adapter_index[None, :],
        axis=1,
    ) * ADAPTER_RANK + lax.rem(lane, ADAPTER_RANK)
    pick = chosen[None, :] == jnp.arange(query_down_maps.shape[1])[:, None]
    is_query = lane < prompts * ADAPTER_RANK
    pick_query = (pick & is_query[None, :]).astype(jnp.bfloat16)
    pick_value = (pick & ~is_query[None, :]).astype(jnp.bfloat16)
    down = (
        jnp.dot(query_down_maps, pick_query, preferred_element_type=jnp.float32)
        + jnp.dot(value_down_maps, pick_value, preferred_element_type=jnp.float32)
    ).astype(jnp.bfloat16)
    query_up = jnp.dot(
        pick_query.T, query_up_maps, preferred_element_type=jnp.float32
    ).astype(jnp.bfloat16)
    value_up = jnp.dot(
        pick_value.T, value_up_maps, preferred_element_type=jnp.float32
    ).astype(jnp.bfloat16)
    gain = input_norm_gain.reshape(peers, 1, width)
    across, gain, cosine, sine, prompt_mask, down, query_up, value_up = lax.optimization_barrier(
        (across, gain, cosine, sine, prompt_mask, down, query_up, value_up)
    )
    far = flip(across, 1)

    def full(shape):
        return pl.BlockSpec(shape, lambda j, s: (0,) * len(shape))

    def weight(columns):
        return pl.BlockSpec((width, columns), lambda j, s: (s[0] ^ j, 0))

    places = jnp.stack([tp_index, layer]).astype(jnp.int32)
    lanes = lane.shape[0]
    key_value, normed = pl.pallas_call(
        project_kernel,
        grid_spec=pltpu.PrefetchScalarGridSpec(
            num_scalar_prefetch=1,
            grid=(peers,),
            in_specs=[full((row_count, width))] * 4
            + [full((peers, 1, width))]
            + [full((row_count, HEAD))] * 2
            + [full((row_count, lanes))]
            + [weight(features)] * 2
            + [weight(lanes), full((lanes, features))],
            out_specs=[
                full((LAYERS, 2, row_count, HEAD)),
                full((peers, row_count, width)),
            ],
            scratch_shapes=[pltpu.VMEM((row_count, features), jnp.float32)] * 2
            + [pltpu.VMEM((row_count, lanes), jnp.float32)],
        ),
        out_shape=[
            jax.ShapeDtypeStruct((LAYERS, 2, row_count, HEAD), jnp.bfloat16),
            jax.ShapeDtypeStruct((peers, row_count, width), jnp.bfloat16),
        ],
        compiler_params=pltpu.CompilerParams(vmem_limit_bytes=48 * 1024 * 1024),
        name="project",
    )(
        places,
        tokens,
        near,
        across,
        far,
        gain,
        cosine,
        sine,
        prompt_mask,
        key_weight,
        value_weight,
        down,
        value_up,
    )
    queries = pl.pallas_call(
        query_kernel,
        grid_spec=pltpu.PrefetchScalarGridSpec(
            num_scalar_prefetch=1,
            grid=(peers,),
            in_specs=[pl.BlockSpec((1, row_count, width), lambda j, s: (j, 0, 0))]
            + [full((row_count, HEAD))] * 2
            + [full((row_count, lanes)), weight(features), weight(lanes)]
            + [full((lanes, features))],
            out_specs=full((LAYERS, row_count, HEAD)),
            scratch_shapes=[
                pltpu.VMEM((row_count, features), jnp.float32),
                pltpu.VMEM((row_count, lanes), jnp.float32),
            ],
        ),
        out_shape=jax.ShapeDtypeStruct((LAYERS, row_count, HEAD), jnp.bfloat16),
        compiler_params=pltpu.CompilerParams(vmem_limit_bytes=48 * 1024 * 1024),
        cost_estimate=pl.CostEstimate(
            flops=2 * row_count * depth * (features + lanes),
            bytes_accessed=2 * depth * (row_count + features),
            transcendentals=0,
        ),
        name="project_queries",
    )(places, normed, cosine, sine, prompt_mask, query_weight, down, query_up)

    def along(array, distance):
        pairs = [
            (z * COLUMNS + y, (z + distance) % LAYERS * COLUMNS + y)
            for z in range(LAYERS)
            for y in range(COLUMNS)
        ]
        return lax.ppermute(array, "req", pairs)

    def swap(array):
        return lax.ppermute(array, "req", [(i, i ^ 1) for i in range(LAYERS * COLUMNS)])

    arrived = {s: along(key_value[s], s) for s in (2, 1, 3)}
    own_swapped = swap(key_value[0])
    queries, first, second, third = lax.optimization_barrier(
        (queries, arrived[1], arrived[2], arrived[3])
    )
    arrived = {1: first, 2: second, 3: third}
    other = jnp.stack([own_swapped] + [swap(arrived[s]) for s in range(1, LAYERS)])
    mine = jnp.stack([key_value[0]] + [arrived[s] for s in range(1, LAYERS)])
    queries = jnp.stack(
        [queries[0]] + [along(queries[s], s) for s in range(1, LAYERS)]
    )
    attended = pl.pallas_call(
        attend_kernel,
        grid_spec=pltpu.PrefetchScalarGridSpec(
            num_scalar_prefetch=1,
            grid=(LAYERS,),
            in_specs=[
                full((LAYERS, row_count, HEAD)),
                full((LAYERS, 2, row_count, HEAD)),
                full((LAYERS, 2, row_count, HEAD)),
            ],
            out_specs=pl.BlockSpec((1, row_count, HEAD), lambda j, s: (j, 0, 0)),
            scratch_shapes=[
                pltpu.VMEM((row_count, 1), jnp.float32),
                pltpu.VMEM((row_count, 1), jnp.float32),
                pltpu.VMEM((row_count, HEAD), jnp.float32),
            ],
        ),
        out_shape=jax.ShapeDtypeStruct((LAYERS, row_count, HEAD), jnp.bfloat16),
        compiler_params=pltpu.CompilerParams(vmem_limit_bytes=48 * 1024 * 1024),
        name="attend",
    )(
        jnp.concatenate([jnp.stack([layer, column]).astype(jnp.int32), lengths]),
        queries,
        mine,
        other,
    )
    parts = [attended[0]] + [along(attended[s], LAYERS - s) for s in range(1, LAYERS)]
    parts = jnp.stack(parts)
    slots = lax.rem(jnp.arange(LAYERS, dtype=jnp.int32) - layer + LAYERS, LAYERS)
    return jnp.concatenate([parts[slots[h]] for h in range(LAYERS)], axis=1)


def solution(mesh):
    in_specs = (
        P("req", "tp"),
        P(),
        P(None, "tp"),
        P(None, "tp"),
        P(None, "tp"),
        P(),
        P(),
        P(None, "tp"),
        P(None, "tp"),
        P(),
        P(),
    )
    out_specs = P("req", "tp")
    fast = mesh.shape["req"] == LAYERS * COLUMNS and mesh.shape["tp"] == 4
    chosen = fast_body if fast else body
    return jax.shard_map(
        chosen, mesh=mesh, in_specs=in_specs, out_specs=out_specs, check_vma=False
    )
```
